256 devices in a mesh: tmpl: 64 (over x_hi, y, z), chan: 4 (over x_lo, core).
Axes of the slice: x: 4 (x_hi: 2, x_lo: 2; x = x_hi * 2 + x_lo), y: 4, z: 8, core: 2. Of those that a mesh axis runs over, the one named last changes fastest.
Arguments:
- data_spec: float32 [2, 600, 1024], P(None, 'chan', 'tmpl')
- tmpl_spec: float32 [2, 256, 600, 1024], P(None, 'tmpl', 'chan'), may hold values from -6 to 6
- shifts: int32 [256, 600], P('tmpl', 'chan'), may hold values from 0 to 255
- mask: int32 [256, 600], P('tmpl', 'chan'), may hold values 0 or 1
Outputs:
- stack: float32 [256, 3072], P('tmpl', 'chan')
The draws below stay inside these ranges and needn't reach their ends.
All inputs are finite; a program needn't handle non-finite values. No bound on the sum of `mask` on one device may be relied on, other than what follows from the above.
Results may differ from the reference program's by a relative error of at most 0.0003.
Values sent between devices are 32-bit elements; how exact they have to be, the bound alone decides.
No kernel may reach another device: no remote copies, remote signals or barrier semaphores. Data moves between devices by JAX's collectives and lax.ppermute only.
A program may use at most 64 MiB of HBM per device.

```python
import math
import jax
import jax.numpy as jnp
from jax import lax

FREQS = 1024
FIRST = 128
NFFT = 4096
LAGS = 3072
MAXSHIFT = 256
TEMPLATES = 256
CHANNELS = 600


def draw_data_spec(key, part):
    key = jax.random.fold_in(key, 11)
    first_key, second_key = jax.random.split(key)
    base = jnp.clip(jax.random.normal(first_key, (2, CHANNELS, FREQS), jnp.float32), -6.0, 6.0)
    level = jnp.exp(jax.random.uniform(second_key, (CHANNELS,), jnp.float32, 0.0, math.log(10.0)))
    ramp = 1.0 + 2.0 * jnp.arange(FREQS, dtype=jnp.float32) / (FREQS - 1)
    return (base * level[None, :, None] * ramp[None, None, :]).astype(jnp.float32)


def with_ends(entries, rng, low, top_value):
    index_at = [jax.random.randint(jax.random.fold_in(rng, axis), (), 0, length) for axis, length in enumerate(entries.shape)]
    widest = entries.shape.index(max(entries.shape))
    next_to = index_at[:widest] + [(index_at[widest] + 1) % entries.shape[widest]] + index_at[widest + 1:]
    return entries.at[tuple(index_at)].set(low).at[tuple(next_to)].set(top_value)


def block_levels(own_key, dims, cuts, smallest, largest):
    level = 1.0
    for dim, parts in cuts:
        heights = jax.random.uniform(jax.random.fold_in(jax.random.fold_in(own_key, 6), dim), (parts,), jnp.float32, smallest / len(cuts), largest / len(cuts))
        level = level * jnp.repeat(jnp.exp(heights), dims[dim] // parts).reshape((-1,) + (1,) * (len(dims) - 1 - dim))
    return level


def gaussian(key, extent, width, most, cuts=(), held_as=jnp.bfloat16):
    array = width * jax.random.normal(key, extent, jnp.float32)
    if cuts:
        array = array * block_levels(key, extent, cuts, -0.22, 0.18)
    return jnp.clip(array, -most, most).astype(held_as)


def setup_inputs(seed: int = 0) -> dict:
    keys = jax.random.split(jax.random.key(seed), 5)
    return {
        "data_spec": draw_data_spec(jax.random.fold_in(keys[4], 71), 0),
        "tmpl_spec": gaussian(keys[1], (2, TEMPLATES, CHANNELS, FREQS), 1.0, 6.0, ((1, 64), (2, 4)), jnp.float32),
        "shifts": with_ends(jax.random.randint(keys[2], (TEMPLATES, CHANNELS), 0, MAXSHIFT), jax.random.fold_in(keys[2], 1), 0, MAXSHIFT - 1).astype(jnp.int32),
        "mask": with_ends((jax.random.randint(keys[3], (TEMPLATES, CHANNELS), 0, 2) < 1).astype(jnp.int32), jax.random.fold_in(keys[3], 1), 0, 1),
    }


full_turn = 2.0 * math.pi

def reference(data_spec, tmpl_spec, shifts, mask):
    data_re = data_spec[0]
    data_im = data_spec[1]
    power = lax.optimization_barrier(jnp.sum(data_re * data_re + data_im * data_im, axis=1)) / FREQS
    data_scale = 1.0 / jnp.sqrt(power + 1e-06)
    bins = FIRST + jnp.arange(FREQS, dtype=jnp.int32)

    def one_template(items):
        spec, moves, used = items
        spec_re = spec[0]
        spec_im = spec[1]
        tpower = lax.optimization_barrier(jnp.sum(spec_re * spec_re + spec_im * spec_im, axis=1)) / FREQS
        weight = used.astype(jnp.float32) / jnp.sqrt(tpower + 1e-06) * data_scale
        turns = bins[None, :] * moves[:, None] % NFFT
        phase = full_turn * turns.astype(jnp.float32) / NFFT
        prod_re = spec_re * data_re + spec_im * data_im
        prod_im = spec_re * data_im - spec_im * data_re
        shift_re = prod_re * jnp.cos(phase) - prod_im * jnp.sin(phase)
        shift_im = prod_re * jnp.sin(phase) + prod_im * jnp.cos(phase)
        return jnp.stack([lax.optimization_barrier(jnp.sum(weight[:, None] * shift_re, axis=0)), lax.optimization_barrier(jnp.sum(weight[:, None] * shift_im, axis=0))])
    network = lax.map(one_template, (jnp.moveaxis(tmpl_spec, 1, 0), shifts, mask))
    lags = jnp.arange(LAGS, dtype=jnp.int32)
    turns = bins[:, None] * lags[None, :] % NFFT
    angle = full_turn * turns.astype(jnp.float32) / NFFT
    high = lax.Precision.HIGHEST
    stack = jnp.dot(network[:, 0], jnp.cos(angle), precision=high) - jnp.dot(network[:, 1], jnp.sin(angle), precision=high)
    return stack / FREQS
```

```python
import math

import jax
import jax.numpy as jnp
import numpy as np
from jax import lax
from jax.experimental import pallas as pl
from jax.experimental.pallas import tpu as pltpu
from jax.sharding import PartitionSpec as P

FREQS = 1024
FIRST = 128
NFFT = 4096
LAGS = 3072
CHANS = 150
ROWS = 152
TMPL = 4
XH, YS, ZS = 2, 4, 8

VMEM = pl.BlockSpec(memory_space=pltpu.VMEM)
HIGH = lax.Precision.HIGHEST
PARAMS = pltpu.CompilerParams(vmem_limit_bytes=48 << 20)


def from_offset(x, dx=0, dy=0, dz=0):
    pairs = []
    for i in range(XH * YS * ZS):
        a, b, c = i // (YS * ZS), i // ZS % YS, i % ZS
        src = (a + dx) % XH * (YS * ZS) + (b + dy) % YS * ZS + (c + dz) % ZS
        pairs.append((src, i))
    return lax.ppermute(x, "tmpl", pairs)


def sincos(turns):
    moved = turns + 512
    quad = moved >> 10
    theta = ((moved & 1023) - 512).astype(jnp.float32) * (2.0 * math.pi / NFFT)
    sq = theta * theta
    sin = theta * (1.0 + sq * (-1.0 / 6 + sq * (1.0 / 120 + sq * (-1.0 / 5040))))
    cos = 1.0 + sq * (-0.5 + sq * (1.0 / 24 + sq * (-1.0 / 720 + sq * (1.0 / 40320))))
    odd = (quad & 1) != 0
    c = jnp.where(odd, sin, cos)
    s = jnp.where(odd, cos, sin)
    c = jnp.where(((quad + 1) & 2) != 0, -c, c)
    s = jnp.where((quad & 2) != 0, -s, s)
    return c, s


def template_kernel(spec_ref, shift_ref, mask_ref, out_ref, code_ref):
    code = shift_ref[...] + 256 * mask_ref[...]
    code_ref[0:4, 0:CHANS] = code
    code_ref[4:8, 0:CHANS] = code
    row = lax.broadcasted_iota(jnp.int32, (8, 128), 0)
    lane = lax.broadcasted_iota(jnp.int32, (8, 128), 1)
    first_bin = FIRST * (row // 4 + 1) + lane

    def channel(c, codes, at):
        col = jnp.broadcast_to(pltpu.roll(codes, (128 - at) % 128, 1)[:, 0:1], (8, 128))
        move = col & 255
        used = (col >> 8).astype(jnp.float32)
        er, ei = sincos((first_bin * move) & (NFFT - 1))
        wr, wi = sincos((256 * move) & (NFFT - 1))
        re = [spec_ref[0, c, m] for m in range(4)]
        im = [spec_ref[1, c, m] for m in range(4)]
        power = sum(a * a + b * b for a, b in zip(re, im))
        power = jnp.broadcast_to(jnp.sum(power, axis=1, keepdims=True), (8, 128))
        power = power + pltpu.roll(power, 4, 0)
        weight = used / jnp.sqrt(power * (1.0 / FREQS) + 1e-06)
        er, ei = er * weight, ei * weight
        for m in range(4):
            out_ref[c, 0, m] = re[m] * er + im[m] * ei
            out_ref[c, 1, m] = re[m] * ei - im[m] * er
            if m < 3:
                er, ei = er * wr - ei * wi, er * wi + ei * wr

    for start, count, unroll in ((0, 128, 4), (128, CHANS - 128, 2)):
        codes = code_ref[:, start : start + 128]

        def step(i, carry, start=start, unroll=unroll, codes=codes):
            for j in range(unroll):
                at = i * unroll + j
                channel(start + at, codes, at)
            return carry

        lax.fori_loop(0, count // unroll, step, 0)


def template_part(tmpl_spec, shifts, mask):
    view = tmpl_spec.reshape(2, TMPL, CHANS, 4, 2, 128).transpose(0, 2, 3, 4, 1, 5)
    view = view.reshape(2, CHANS, 4, 8, 128)
    return pl.pallas_call(
        template_kernel,
        out_shape=jax.ShapeDtypeStruct((CHANS, 2, 4, 8, 128), jnp.float32),
        in_specs=[VMEM] * 3,
        out_specs=VMEM,
        scratch_shapes=[pltpu.VMEM((8, 256), jnp.int32)],
        compiler_params=PARAMS,
    )(view, shifts, mask)


Z_ORDER = (0, 1, -1, 2, -2, 3, 4, -3)


def pack_kernel(*refs):
    parts, out_ref, held = refs[:8], refs[8], refs[9]
    z = lax.axis_index("tmpl") % ZS
    for part, dz in zip(parts, Z_ORDER):
        at = pl.multiple_of(lax.rem(z + dz + ZS, ZS) * 16, 16)
        for k in range(2):
            held[k, pl.ds(at, 16), 0:CHANS] = part[k]
    for k in range(2):
        out_ref[k, 0:128, :] = held[k, :, 0:128].T
        out_ref[k, 128:ROWS, :] = held[k, :, 128:256].T[0 : ROWS - 128]


def gather_z(data_spec):
    own = data_spec.transpose(0, 2, 1)
    up = from_offset(own, dz=1)
    down = from_offset(own, dz=-1)
    up2 = from_offset(own, dz=2)
    down2 = from_offset(own, dz=-2)
    up3 = from_offset(up2, dz=1)
    up4 = from_offset(up2, dz=2)
    down3 = from_offset(down2, dz=-1)
    return pl.pallas_call(
        pack_kernel,
        out_shape=jax.ShapeDtypeStruct((2, ROWS, 128), jnp.float32),
        in_specs=[VMEM] * 8,
        out_specs=VMEM,
        scratch_shapes=[pltpu.VMEM((2, 128, 256), jnp.float32)],
        compiler_params=PARAMS,
    )(own, up, down, up2, down2, up3, up4, down3)


XY_ORDER = ((0, 0), (1, 0), (0, 1), (0, -1), (1, 1), (1, -1), (1, 2), (0, 2))


def gather_xy(own):
    ax = from_offset(own, dx=1)
    up = from_offset(own, dy=1)
    down = from_offset(own, dy=-1)
    far = from_offset(ax, dy=2)
    xup = from_offset(up, dx=1)
    xdown = from_offset(down, dx=1)
    re2 = from_offset(up[0], dy=1)
    im2 = from_offset(down[1], dy=-1)
    return own, ax, up, down, xup, xdown, far, re2, im2


def tables():
    kl = np.arange(32)
    fh = np.arange(8)
    a = 2 * np.pi * (np.outer(kl, fh + 1) % 32) / 32
    first = np.zeros((2, TMPL, 32, 2, 4, 2, TMPL))
    for t in range(TMPL):
        c, s = np.cos(a).reshape(32, 4, 2), np.sin(a).reshape(32, 4, 2)
        first[0, t, :, 0, :, :, t] = c
        first[0, t, :, 1, :, :, t] = -s
        first[1, t, :, 0, :, :, t] = s
        first[1, t, :, 1, :, :, t] = c
    fl = np.arange(128)
    b = np.tile(2 * np.pi * np.outer(kl, fl) / NFFT, (TMPL, 1))
    kh = (4 * np.arange(24)[None, :] + np.arange(4)[:, None]).reshape(96)
    g = 2 * np.pi * (np.outer(kh, fl) % 128) / 128
    rows = [first.reshape(256, 64)]
    twist = np.stack([np.cos(b), np.sin(b)])
    last = np.stack([np.cos(g), -np.sin(g)]) / FREQS
    return tuple(np.asarray(v, np.float32) for v in (rows[0], twist, last))


def network_kernel(*refs):
    spec_ref = refs[0]
    blocks = refs[1:8]
    re2_ref, im2_ref, first_ref, twist_ref, last_ref = refs[8:13]
    keep_ref, send_ref, data_ref, piece_ref = refs[13:]
    me = lax.axis_index("tmpl")
    x, y = me // (YS * ZS), me // ZS % YS

    def block(q, k):
        if q < 7:
            return blocks[q][k]
        return (re2_ref, im2_ref)[k][...]

    power = None
    for q in range(8):
        re, im = block(q, 0), block(q, 1)
        one = re * re + im * im
        power = one if power is None else power + one
    power = jnp.sum(power, axis=1, keepdims=True)
    scale = jnp.broadcast_to(1.0 / jnp.sqrt(power * (1.0 / FREQS) + 1e-06), (ROWS, 128))
    for q, (dx, dy) in enumerate(XY_ORDER):
        group = lax.rem(x + dx, XH) * YS + lax.rem(y + dy + YS, YS)
        for k in range(2):
            data_ref[group, k] = block(q, k) * scale

    lower = lax.broadcasted_iota(jnp.int32, (8, 128), 0) < 4

    def channel(c, acc):
        acc = list(acc)
        for m in range(4):
            d = []
            for k in range(2):
                one = jnp.broadcast_to(data_ref[2 * m, k, pl.ds(c, 1), :], (8, 128))
                two = jnp.broadcast_to(data_ref[2 * m + 1, k, pl.ds(c, 1), :], (8, 128))
                d.append(jnp.where(lower, one, two))
            tr, ti = spec_ref[c, 0, m], spec_ref[c, 1, m]
            acc[m] = acc[m] + (tr * d[0] - ti * d[1])
            acc[4 + m] = acc[4 + m] + (tr * d[1] + ti * d[0])
        return tuple(acc)

    zero = jnp.zeros((8, 128), jnp.float32)
    acc = lax.fori_loop(0, CHANS, channel, (zero,) * 8, unroll=5)
    spectra = jnp.concatenate(acc, axis=0)
    mixed = jnp.dot(first_ref[...], spectra, precision=HIGH, preferred_element_type=jnp.float32)
    yr, yi = mixed[0:128], mixed[128:256]
    tc, ts = twist_ref[0], twist_ref[1]
    zr, zi = yr * tc - yi * ts, yr * ts + yi * tc
    dims = (((1,), (1,)), ((), ()))
    lags = lax.dot_general(last_ref[0], zr, dims, precision=HIGH, preferred_element_type=jnp.float32)
    lags = lags + lax.dot_general(last_ref[1], zi, dims, precision=HIGH, preferred_element_type=jnp.float32)
    lane = lax.broadcasted_iota(jnp.int32, (24, 128), 1) // 32
    chan = lax.axis_index("chan")
    for t in range(TMPL):
        out = None
        for r in range(4):
            part = lags[24 * r : 24 * r + 24]
            if (r - t) % 4:
                part = pltpu.roll(part, (r - t) % 4 * 32, 1)
            out = part if out is None else jnp.where(lane == r, part, out)
        for j in range(4):
            for g in range(6):
                piece_ref[j ^ chan, t : t + 1, g * 128 : (g + 1) * 128] = out[6 * j + g : 6 * j + g + 1]
    keep_ref[0] = piece_ref[0]
    keep_ref[1] = piece_ref[2]
    send_ref[0] = piece_ref[1]
    send_ref[1] = piece_ref[3]


def network_part(spectra, blocks):
    lag_dev = LAGS // 4
    shape = jax.ShapeDtypeStruct((2, TMPL, lag_dev), jnp.float32)
    return pl.pallas_call(
        network_kernel,
        out_shape=(shape, shape),
        in_specs=[VMEM] * 13,
        out_specs=(VMEM, VMEM),
        scratch_shapes=[
            pltpu.VMEM((8, 2, ROWS, 128), jnp.float32),
            pltpu.VMEM((4, TMPL, lag_dev), jnp.float32),
        ],
        compiler_params=PARAMS,
    )(spectra, *blocks, *tables())


def on_device(data_spec, tmpl_spec, shifts, mask):
    spectra = template_part(tmpl_spec, shifts, mask)
    blocks = gather_xy(gather_z(data_spec))
    keep, send = network_part(spectra, blocks)
    got = lax.ppermute(send, "chan", [(i, i ^ 1) for i in range(4)])
    other = lax.ppermute(keep[1] + got[1], "chan", [(i, i ^ 2) for i in range(4)])
    return keep[0] + got[0] + other


def solution(mesh):
    return jax.shard_map(
        on_device,
        mesh=mesh,
        in_specs=(
            P(None, "chan", "tmpl"),
            P(None, "tmpl", "chan", None),
            P("tmpl", "chan"),
            P("tmpl", "chan"),
        ),
        out_specs=P("tmpl", "chan"),
        check_vma=False,
    )
```

```python
import functools
import math

import jax
import jax.numpy as jnp
import numpy as np
from jax import lax
from jax.experimental import pallas as pl
from jax.experimental.pallas import tpu as pltpu
from jax.sharding import PartitionSpec as P

FREQS = 1024
FIRST = 128
NFFT = 4096
LAGS = 3072
CHANS = 150
ROWS = 152
TMPL = 4
XH, YS, ZS = 2, 4, 8

VMEM = pl.BlockSpec(memory_space=pltpu.VMEM)
HIGH = lax.Precision.HIGHEST
PARAMS = pltpu.CompilerParams(vmem_limit_bytes=16 << 20)
LARGE = pltpu.CompilerParams(vmem_limit_bytes=40 << 20)


def from_offset(x, dx=0, dy=0, dz=0):
    pairs = []
    for i in range(XH * YS * ZS):
        a, b, c = i // (YS * ZS), i // ZS % YS, i % ZS
        src = (a + dx) % XH * (YS * ZS) + (b + dy) % YS * ZS + (c + dz) % ZS
        pairs.append((src, i))
    return lax.ppermute(x, "tmpl", pairs)


def half_turn_fit():
    x = np.cos(np.pi * (np.arange(400) + 0.5) / 400) * 0.25 + 0.25
    r = np.sqrt(x)
    even = np.polynomial.Chebyshev.fit(x, np.cos(np.pi * r), 5, domain=[0, 0.5])
    odd = np.polynomial.Chebyshev.fit(x, np.sin(np.pi * r) / r, 5, domain=[0, 0.5])
    return [[float(v) for v in p.convert(kind=np.polynomial.Polynomial).coef] for p in (even, odd)]


COS_FIT, SIN_FIT = half_turn_fit()


def sincos(turns):
    near = jnp.floor(turns + 0.5)
    r = turns - near
    half = near * 0.5
    sign = 1.0 - 4.0 * (half - jnp.floor(half))
    sq = r * r
    c, s = COS_FIT[-1], SIN_FIT[-1]
    for a, b in zip(COS_FIT[-2::-1], SIN_FIT[-2::-1]):
        c, s = c * sq + a, s * sq + b
    return sign, c, s * r


STEP = 30
STEPS = CHANS // STEP


def template_kernel(spec_ref, code_ref, after_hbm, out_ref, pair_ref, wide_ref, weight_ref):
    row = lax.broadcasted_iota(jnp.int32, (8, 128), 0)
    lane = lax.broadcasted_iota(jnp.int32, (8, 128), 1)
    first_bin = (FIRST * (row // 4 + 1) + lane).astype(jnp.float32) * (2.0 / NFFT)

    base = pl.program_id(0) * STEP

    @pl.when(pl.program_id(0) == 0)
    def _():
        pair_ref[0:4, 0:CHANS] = code_ref[...]
        pair_ref[4:8, 0:CHANS] = code_ref[...]
        for start in (0, 128):
            codes = pair_ref[:, start : start + 128]
            sign, wr, wi = sincos(codes * (2.0 * 2 * FIRST / NFFT))
            wr, wi = wr * sign, wi * sign
            for at in range(min(128, CHANS - start)):
                for k, part in enumerate((codes, wr, wi)):
                    wide_ref[start + at, k] = jnp.broadcast_to(part[:, at : at + 1], (8, 128))

    def weigh(c):
        power = None
        for m in range(4):
            re, im = spec_ref[0, c, m], spec_ref[1, c, m]
            one = re * re + im * im
            power = one if power is None else power + one
        power = jnp.broadcast_to(jnp.sum(power, axis=1, keepdims=True), (8, 128))
        power = power + pltpu.roll(power, 4, 0)
        weight = lax.rsqrt(power * (1.0 / FREQS) + 1e-06)
        weight_ref[c] = jnp.where(wide_ref[base + c, 0] >= NFFT, weight, 0.0)

    def phase(c):
        sign, er, ei = sincos(first_bin * wide_ref[base + c, 0])
        wr, wi = wide_ref[base + c, 1], wide_ref[base + c, 2]
        weight = weight_ref[c] * sign
        er, ei = er * weight, ei * weight
        for m in range(4):
            re, im = spec_ref[0, c, m], spec_ref[1, c, m]
            out_ref[c, 0, m] = re * er + im * ei
            out_ref[c, 1, m] = re * ei - im * er
            if m < 3:
                er, ei = er * wr - ei * wi, er * wi + ei * wr

    for body, unroll in ((weigh, 10), (phase, 5)):

        def step(j, carry, body=body, unroll=unroll):
            for k in range(unroll):
                body(j * unroll + k)
            return carry

        lax.fori_loop(0, STEP // unroll, step, 0)


def template_view(tmpl_spec):
    view = tmpl_spec.reshape(2, TMPL, CHANS, 4, 2, 128).transpose(0, 2, 3, 4, 1, 5)
    return view.reshape(2, CHANS, 4, 8, 128)


def template_part(tmpl_spec, code, after):
    return pl.pallas_call(
        template_kernel,
        grid=(STEPS,),
        out_shape=jax.ShapeDtypeStruct((CHANS, 2, 4, 8, 128), jnp.float32),
        in_specs=[
            pl.BlockSpec((2, STEP, 4, 8, 128), lambda i: (0, i, 0, 0, 0)),
            VMEM,
            pl.BlockSpec(memory_space=pl.ANY),
        ],
        out_specs=pl.BlockSpec((STEP, 2, 4, 8, 128), lambda i: (i, 0, 0, 0, 0)),
        scratch_shapes=[
            pltpu.VMEM((8, 256), jnp.float32),
            pltpu.VMEM((CHANS, 3, 8, 128), jnp.float32),
            pltpu.VMEM((STEP, 8, 128), jnp.float32),
        ],
        compiler_params=LARGE,
    )(template_view(tmpl_spec), code, after)


REST = CHANS - 128
DENSE = 80


def dense_kernel(own_ref, other_ref, out_ref):
    out_ref[64:DENSE, :] = jnp.zeros((DENSE - 64, 128), jnp.float32)
    for j in range(4):
        ref = (own_ref, other_ref)[j // 2]
        out_ref[16 * j : 16 * j + 16, :] = ref[j % 2, :, 0:128]
        out_ref[64:DENSE, 32 * j : 32 * j + REST] = ref[j % 2, :, 128:CHANS]


Z_ORDER = (0, 1, -1, 2, -2, 3, 4, -3)


def pack_kernel(*refs):
    parts, out_ref, held = refs[:8], refs[8], refs[9]
    z = lax.axis_index("tmpl") % ZS
    for part, dz in zip(parts, Z_ORDER):
        at = pl.multiple_of(lax.rem(z + dz + ZS, ZS) * 16, 16)
        for j in range(5):
            held[j, pl.ds(at, 16), :] = part[16 * j : 16 * j + 16, :]
    rest = held[4].T
    for j in range(4):
        out_ref[j // 2, j % 2, 0:128, :] = held[j].T
        out_ref[j // 2, j % 2, 128:ROWS, :] = rest[32 * j : 32 * j + ROWS - 128]


def gather_xz(data_spec):
    raw = data_spec.transpose(0, 2, 1)
    own = pl.pallas_call(
        dense_kernel,
        out_shape=jax.ShapeDtypeStruct((DENSE, 128), jnp.float32),
        in_specs=[VMEM] * 2,
        out_specs=VMEM,
        compiler_params=PARAMS,
    )(raw, from_offset(raw, dx=1))
    up = from_offset(own, dz=1)
    down = from_offset(own, dz=-1)
    up2 = from_offset(own, dz=2)
    down2 = from_offset(own, dz=-2)
    up3 = from_offset(up2, dz=1)
    up4 = from_offset(up2, dz=2)
    down3 = from_offset(down2, dz=-1)
    return pl.pallas_call(
        pack_kernel,
        out_shape=jax.ShapeDtypeStruct((2, 2, ROWS, 128), jnp.float32),
        in_specs=[VMEM] * 8,
        out_specs=VMEM,
        scratch_shapes=[pltpu.VMEM((5, 128, 128), jnp.float32)],
        compiler_params=PARAMS,
    )(own, up, down, up2, down2, up3, up4, down3)


Y_ORDER = (0, 1, -1, 2)


def gather_y(own):
    return (own,) + tuple(from_offset(own, dy=dy) for dy in Y_ORDER[1:])


def tables():
    kl = np.arange(32)
    fh = np.arange(8)
    a = 2 * np.pi * (np.outer(kl, fh + 1) % 32) / 32
    first = np.zeros((2, TMPL, 32, 2, 4, 2, TMPL))
    for t in range(TMPL):
        c, s = np.cos(a).reshape(32, 4, 2), np.sin(a).reshape(32, 4, 2)
        first[0, t, :, 0, :, :, t] = c
        first[0, t, :, 1, :, :, t] = -s
        first[1, t, :, 0, :, :, t] = s
        first[1, t, :, 1, :, :, t] = c
    fl = np.arange(128)
    b = np.tile(2 * np.pi * np.outer(kl, fl) / NFFT, (TMPL, 1))
    kh = (4 * np.arange(24)[None, :] + np.arange(4)[:, None]).reshape(96)
    g = 2 * np.pi * (np.outer(kh, fl) % 128) / 128
    rows = [first.reshape(256, 64)]
    twist = np.stack([np.cos(b), np.sin(b)])
    last = np.stack([np.cos(g), -np.sin(g)]) / FREQS
    return tuple(np.asarray(v, np.float32) for v in (rows[0], twist, last))


def network_kernel(*refs):
    spec_ref, blocks = refs[0], refs[1:5]
    first_ref, twist_ref, last_ref, keep_ref, send_ref, data_ref, piece_ref, acc_ref = refs[5:]
    pl.when(pl.program_id(0) == 0)(functools.partial(scale_data, blocks, data_ref, acc_ref))
    base = pl.program_id(0) * STEP
    lower = lax.broadcasted_iota(jnp.int32, (8, 128), 0) < 4

    def channel(c, acc):
        acc = list(acc)
        for m in range(4):
            d = []
            for k in range(2):
                one = jnp.broadcast_to(data_ref[2 * m, k, pl.ds(base + c, 1), :], (8, 128))
                two = jnp.broadcast_to(data_ref[2 * m + 1, k, pl.ds(base + c, 1), :], (8, 128))
                d.append(jnp.where(lower, one, two))
            tr, ti = spec_ref[c, 0, m], spec_ref[c, 1, m]
            acc[m] = acc[m] + (tr * d[0] - ti * d[1])
            acc[4 + m] = acc[4 + m] + (tr * d[1] + ti * d[0])
        return tuple(acc)

    acc = lax.fori_loop(0, STEP, channel, tuple(acc_ref[i] for i in range(8)), unroll=5)
    for i in range(8):
        acc_ref[i] = acc[i]

    @pl.when(pl.program_id(0) == STEPS - 1)
    def _():
        to_lags(acc, first_ref, twist_ref, last_ref, piece_ref)
        keep_ref[0] = piece_ref[0]
        keep_ref[1] = piece_ref[2]
        send_ref[0] = piece_ref[1]
        send_ref[1] = piece_ref[3]


def scale_data(blocks, data_ref, acc_ref):
    acc_ref[...] = jnp.zeros_like(acc_ref)
    me = lax.axis_index("tmpl")
    x, y = me // (YS * ZS), me // ZS % YS

    power = None
    for block in blocks:
        for dx in range(XH):
            re, im = block[dx, 0], block[dx, 1]
            one = re * re + im * im
            power = one if power is None else power + one
    power = jnp.sum(power, axis=1, keepdims=True)
    scale = jnp.broadcast_to(lax.rsqrt(power * (1.0 / FREQS) + 1e-06), (ROWS, 128))
    for block, dy in zip(blocks, Y_ORDER):
        for dx in range(XH):
            group = lax.rem(x + dx, XH) * YS + lax.rem(y + dy + YS, YS)
            for k in range(2):
                data_ref[group, k] = block[dx, k] * scale


def to_lags(acc, first_ref, twist_ref, last_ref, piece_ref):
    spectra = jnp.concatenate(acc, axis=0)
    mixed = jnp.dot(first_ref[...], spectra, precision=HIGH, preferred_element_type=jnp.float32)
    yr, yi = mixed[0:128], mixed[128:256]
    tc, ts = twist_ref[0], twist_ref[1]
    zr, zi = yr * tc - yi * ts, yr * ts + yi * tc
    dims = (((1,), (1,)), ((), ()))
    lags = lax.dot_general(last_ref[0], zr, dims, precision=HIGH, preferred_element_type=jnp.float32)
    lags = lags + lax.dot_general(last_ref[1], zi, dims, precision=HIGH, preferred_element_type=jnp.float32)
    lane = lax.broadcasted_iota(jnp.int32, (24, 128), 1) // 32
    chan = lax.axis_index("chan")
    for t in range(TMPL):
        out = None
        for r in range(4):
            part = lags[24 * r : 24 * r + 24]
            if (r - t) % 4:
                part = pltpu.roll(part, (r - t) % 4 * 32, 1)
            out = part if out is None else jnp.where(lane == r, part, out)
        for j in range(4):
            for g in range(6):
                piece_ref[j ^ chan, t : t + 1, g * 128 : (g + 1) * 128] = out[6 * j + g : 6 * j + g + 1]


def network_part(spectra, blocks):
    lag_dev = LAGS // 4
    shape = jax.ShapeDtypeStruct((2, TMPL, lag_dev), jnp.float32)
    return pl.pallas_call(
        network_kernel,
        grid=(STEPS,),
        out_shape=(shape, shape),
        in_specs=[pl.BlockSpec((STEP, 2, 4, 8, 128), lambda i: (i, 0, 0, 0, 0))] + [VMEM] * 7,
        out_specs=(VMEM, VMEM),
        scratch_shapes=[
            pltpu.VMEM((8, 2, ROWS, 128), jnp.float32),
            pltpu.VMEM((4, TMPL, lag_dev), jnp.float32),
            pltpu.VMEM((8, 8, 128), jnp.float32),
        ],
        compiler_params=PARAMS,
    )(spectra, *blocks, *tables())


def on_device(data_spec, tmpl_spec, shifts, mask):
    own = gather_xz(data_spec)
    blocks = gather_y(own)
    code = (shifts + NFFT * mask).astype(jnp.float32)
    spectra = template_part(tmpl_spec, code, own)
    keep, send = network_part(spectra, blocks)
    got = lax.ppermute(send, "chan", [(i, i ^ 1) for i in range(4)])
    other = lax.ppermute(keep[1] + got[1], "chan", [(i, i ^ 2) for i in range(4)])
    return keep[0] + got[0] + other


def solution(mesh):
    return jax.shard_map(
        on_device,
        mesh=mesh,
        in_specs=(
            P(None, "chan", "tmpl"),
            P(None, "tmpl", "chan", None),
            P("tmpl", "chan"),
            P("tmpl", "chan"),
        ),
        out_specs=P("tmpl", "chan"),
        check_vma=False,
    )
```

```python
import functools
import math

import jax
import jax.numpy as jnp
import numpy as np
from jax import lax
from jax.experimental import pallas as pl
from jax.experimental.pallas import tpu as pltpu
from jax.sharding import PartitionSpec as P

FREQS = 1024
FIRST = 128
NFFT = 4096
LAGS = 3072
CHANS = 150
ROWS = 152
TMPL = 4
XH, YS, ZS = 2, 4, 8

VMEM = pl.BlockSpec(memory_space=pltpu.VMEM)
HIGH = lax.Precision.HIGHEST
PARAMS = pltpu.CompilerParams(vmem_limit_bytes=16 << 20)
LARGE = pltpu.CompilerParams(vmem_limit_bytes=45 << 20)


def from_offset(x, dx=0, dy=0, dz=0):
    pairs = []
    for i in range(XH * YS * ZS):
        a, b, c = i // (YS * ZS), i // ZS % YS, i % ZS
        src = (a + dx) % XH * (YS * ZS) + (b + dy) % YS * ZS + (c + dz) % ZS
        pairs.append((src, i))
    return lax.ppermute(x, "tmpl", pairs)


def half_turn_fit():
    x = np.cos(np.pi * (np.arange(400) + 0.5) / 400) * 0.25 + 0.25
    r = np.sqrt(x)
    even = np.polynomial.Chebyshev.fit(x, np.cos(np.pi * r), 5, domain=[0, 0.5])
    odd = np.polynomial.Chebyshev.fit(x, np.sin(np.pi * r) / r, 5, domain=[0, 0.5])
    return [[float(v) for v in p.convert(kind=np.polynomial.Polynomial).coef] for p in (even, odd)]


COS_FIT, SIN_FIT = half_turn_fit()


def sincos(turns):
    near = jnp.floor(turns + 0.5)
    r = turns - near
    half = near * 0.5
    sign = 1.0 - 4.0 * (half - jnp.floor(half))
    sq = r * r
    c, s = COS_FIT[-1], SIN_FIT[-1]
    for a, b in zip(COS_FIT[-2::-1], SIN_FIT[-2::-1]):
        c, s = c * sq + a, s * sq + b
    return sign, c, s * r


STEP = 50
STEPS = CHANS // STEP


def template_kernel(spec_hbm, wide_ref, after_hbm, out_ref, spec_ref, weight_ref, sems):
    def part(i):
        at = pl.ds(i * STEP, STEP)
        return [pltpu.make_async_copy(spec_hbm.at[k, at], spec_ref.at[k, at], sems.at[i, k]) for k in range(2)]

    for copy in part(0) + part(1):
        copy.start()
    row = lax.broadcasted_iota(jnp.int32, (8, 128), 0)
    lane = lax.broadcasted_iota(jnp.int32, (8, 128), 1)
    first_bin = (FIRST * (row // 4 + 1) + lane).astype(jnp.float32) * (2.0 / NFFT)

    def weigh(c):
        power = None
        for m in range(4):
            re, im = spec_ref[0, c, m], spec_ref[1, c, m]
            one = re * re + im * im
            power = one if power is None else power + one
        power = power + pltpu.roll(power, 4, 0)
        power = jnp.broadcast_to(jnp.sum(power, axis=1, keepdims=True), (8, 128))
        weight = lax.rsqrt(power * (1.0 / FREQS) + 1e-06)
        weight_ref[c] = jnp.where(wide_ref[c, 0] >= NFFT, weight, 0.0)

    def phase(c):
        sign, er, ei = sincos(first_bin * wide_ref[c, 0])
        wr, wi = wide_ref[c, 1], wide_ref[c, 2]
        weight = weight_ref[c] * sign
        er, ei = er * weight, ei * weight
        for m in range(4):
            re, im = spec_ref[0, c, m], spec_ref[1, c, m]
            out_ref[c, 0, m] = re * er + im * ei
            out_ref[c, 1, m] = re * ei - im * er
            if m < 3:
                er, ei = er * wr - ei * wi, er * wi + ei * wr

    for i in range(STEPS):
        for copy in part(i):
            copy.wait()
        if i + 2 < STEPS:
            for copy in part(i + 2):
                copy.start()
        for body, unroll in ((weigh, 25), (phase, 10)):

            def step(j, carry, body=body, unroll=unroll, i=i):
                for k in range(unroll):
                    body(i * STEP + j * unroll + k)
                return carry

            lax.fori_loop(0, STEP // unroll, step, 0)


def template_view(tmpl_spec):
    view = tmpl_spec.reshape(2, TMPL, CHANS, 4, 2, 128).transpose(0, 2, 3, 4, 1, 5)
    return view.reshape(2, CHANS, 4, 8, 128)


def template_part(tmpl_spec, wide, after):
    return pl.pallas_call(
        template_kernel,
        out_shape=jax.ShapeDtypeStruct((CHANS, 2, 4, 8, 128), jnp.float32),
        in_specs=[pl.BlockSpec(memory_space=pl.ANY), VMEM, pl.BlockSpec(memory_space=pl.ANY)],
        out_specs=VMEM,
        scratch_shapes=[
            pltpu.VMEM((2, CHANS, 4, 8, 128), jnp.float32),
            pltpu.VMEM((CHANS, 8, 128), jnp.float32),
            pltpu.SemaphoreType.DMA((STEPS, 2)),
        ],
        compiler_params=LARGE,
    )(template_view(tmpl_spec), wide, after)


REST = CHANS - 128
HELD = 3
REST_AT = HELD * 32
DENSE = REST_AT + 32


def put(j, ref, k, out_ref):
    out_ref[16 * j : 16 * j + 16, :] = ref[k, :, 0:128]
    at = REST_AT + j // 4 * 16
    out_ref[at : at + 16, 32 * (j % 4) : 32 * (j % 4) + REST] = ref[k, :, 128:CHANS]


def early_kernel(raw_ref, code_ref, own_ref, wide_ref, pair_ref):
    own_ref[...] = jnp.zeros((DENSE, 128), jnp.float32)
    for k in range(2):
        put(k, raw_ref, k, own_ref)
    pair_ref[0:4, 0:CHANS] = code_ref[...]
    pair_ref[4:8, 0:CHANS] = code_ref[...]
    for start in (0, 128):
        codes = pair_ref[:, start : start + 128]
        sign, wr, wi = sincos(codes * (2.0 * 2 * FIRST / NFFT))
        wr, wi = wr * sign, wi * sign
        for at in range(min(128, CHANS - start)):
            for k, part in enumerate((codes, wr, wi)):
                wide_ref[start + at, k] = jnp.broadcast_to(part[:, at : at + 1], (8, 128))


def early_part(raw, code):
    return pl.pallas_call(
        early_kernel,
        out_shape=(
            jax.ShapeDtypeStruct((DENSE, 128), jnp.float32),
            jax.ShapeDtypeStruct((CHANS, 3, 8, 128), jnp.float32),
        ),
        in_specs=[VMEM] * 2,
        out_specs=(VMEM, VMEM),
        scratch_shapes=[pltpu.VMEM((8, 256), jnp.float32)],
        compiler_params=PARAMS,
    )(raw, code)


def dense_kernel(own_ref, other_ref, far_ref, out_ref):
    out_ref[...] = own_ref[...]
    for k in range(2):
        put(2 + k, other_ref, k, out_ref)
        put(4 + k, far_ref, k, out_ref)


Z_ORDER = (0, 1, -1, 2, -2, 3, 4, -3)


def pack_kernel(*refs):
    parts, one_ref, far_ref, held = refs[:8], refs[8], refs[9], refs[10]
    z = lax.axis_index("tmpl") % ZS
    for part, dz in zip(parts, Z_ORDER):
        at = pl.multiple_of(lax.rem(z + dz + ZS, ZS) * 16, 16)
        for j in range(DENSE // 16):
            held[j, pl.ds(at, 16), :] = part[16 * j : 16 * j + 16, :]
    rest = [held[j].T for j in range(REST_AT // 16, DENSE // 16)]
    for j in range(2 * HELD):
        out = one_ref.at[j // 2, j % 2] if j < 4 else far_ref.at[j % 2]
        out[0:128, :] = held[j].T
        out[128:ROWS, :] = rest[j // 4][32 * (j % 4) : 32 * (j % 4) + ROWS - 128]


def gather_xz(dense, other, far):
    own = pl.pallas_call(
        dense_kernel,
        out_shape=jax.ShapeDtypeStruct((DENSE, 128), jnp.float32),
        in_specs=[VMEM] * 3,
        out_specs=VMEM,
        compiler_params=PARAMS,
    )(dense, other, far)
    up = from_offset(own, dz=1)
    down = from_offset(own, dz=-1)
    up2 = from_offset(own, dz=2)
    down2 = from_offset(own, dz=-2)
    up3 = from_offset(up2, dz=1)
    up4 = from_offset(up2, dz=2)
    down3 = from_offset(down2, dz=-1)
    return pl.pallas_call(
        pack_kernel,
        out_shape=(
            jax.ShapeDtypeStruct((2, 2, ROWS, 128), jnp.float32),
            jax.ShapeDtypeStruct((2, ROWS, 128), jnp.float32),
        ),
        in_specs=[VMEM] * 8,
        out_specs=(VMEM, VMEM),
        scratch_shapes=[pltpu.VMEM((DENSE // 16, 128, 128), jnp.float32)],
        compiler_params=PARAMS,
    )(own, up, down, up2, down2, up3, up4, down3)


def gather_xy(one, far):
    return one, from_offset(one, dy=1), from_offset(one, dy=-1), far, from_offset(far, dx=1)


def tables():
    kl = np.arange(32)
    fh = np.arange(8)
    a = 2 * np.pi * (np.outer(kl, fh + 1) % 32) / 32
    first = np.zeros((2, TMPL, 32, 2, 4, 2, TMPL))
    for t in range(TMPL):
        c, s = np.cos(a).reshape(32, 4, 2), np.sin(a).reshape(32, 4, 2)
        first[0, t, :, 0, :, :, t] = c
        first[0, t, :, 1, :, :, t] = -s
        first[1, t, :, 0, :, :, t] = s
        first[1, t, :, 1, :, :, t] = c
    fl = np.arange(128)
    b = np.tile(2 * np.pi * np.outer(kl, fl) / NFFT, (TMPL, 1))
    kh = (4 * np.arange(24)[None, :] + np.arange(4)[:, None]).reshape(96)
    g = 2 * np.pi * (np.outer(kh, fl) % 128) / 128
    rows = [first.reshape(256, 64)]
    twist = np.stack([np.cos(b), np.sin(b)])
    last = np.stack([np.cos(g), -np.sin(g)]) / FREQS
    return tuple(np.asarray(v, np.float32) for v in (rows[0], twist, last))


def network_kernel(*refs):
    spec_ref, (one_ref, up_ref, down_ref, far_ref, other_far_ref) = refs[0], refs[1:6]
    first_ref, twist_ref, last_ref, keep_ref, send_ref, data_ref, piece_ref = refs[6:]
    me = lax.axis_index("tmpl")
    x, y = me // (YS * ZS), me // ZS % YS

    views = [(ref.at[dx], dx, dy) for ref, dy in ((one_ref, 0), (up_ref, 1), (down_ref, YS - 1)) for dx in range(XH)]
    views += [(far_ref, 0, 2), (other_far_ref, 1, 2)]
    power = None
    for block, _, _ in views:
        re, im = block[0], block[1]
        part = re * re + im * im
        power = part if power is None else power + part
    power = jnp.sum(power, axis=1, keepdims=True)
    scale = jnp.broadcast_to(lax.rsqrt(power * (1.0 / FREQS) + 1e-06), (ROWS, 128))
    for block, dx, dy in views:
        group = lax.rem(x + dx, XH) * YS + lax.rem(y + dy, YS)
        for k in range(2):
            data_ref[group, k] = block[k] * scale

    lower = lax.broadcasted_iota(jnp.int32, (8, 128), 0) < 4

    def channel(c, acc):
        acc = list(acc)
        for m in range(4):
            d = []
            for k in range(2):
                one = jnp.broadcast_to(data_ref[2 * m, k, pl.ds(c, 1), :], (8, 128))
                two = jnp.broadcast_to(data_ref[2 * m + 1, k, pl.ds(c, 1), :], (8, 128))
                d.append(jnp.where(lower, one, two))
            tr, ti = spec_ref[c, 0, m], spec_ref[c, 1, m]
            acc[m] = acc[m] + (tr * d[0] - ti * d[1])
            acc[4 + m] = acc[4 + m] + (tr * d[1] + ti * d[0])
        return tuple(acc)

    acc = lax.fori_loop(0, CHANS, channel, (jnp.zeros((8, 128), jnp.float32),) * 8, unroll=5)
    to_lags(acc, first_ref, twist_ref, last_ref, piece_ref)
    keep_ref[0] = piece_ref[0]
    keep_ref[1] = piece_ref[2]
    send_ref[0] = piece_ref[1]
    send_ref[1] = piece_ref[3]


def to_lags(acc, first_ref, twist_ref, last_ref, piece_ref):
    spectra = jnp.concatenate(acc, axis=0)
    mixed = jnp.dot(first_ref[...], spectra, precision=HIGH, preferred_element_type=jnp.float32)
    yr, yi = mixed[0:128], mixed[128:256]
    tc, ts = twist_ref[0], twist_ref[1]
    zr, zi = yr * tc - yi * ts, yr * ts + yi * tc
    dims = (((1,), (1,)), ((), ()))
    lags = lax.dot_general(last_ref[0], zr, dims, precision=HIGH, preferred_element_type=jnp.float32)
    lags = lags + lax.dot_general(last_ref[1], zi, dims, precision=HIGH, preferred_element_type=jnp.float32)
    lane = lax.broadcasted_iota(jnp.int32, (24, 128), 1) // 32
    chan = lax.axis_index("chan")
    for t in range(TMPL):
        out = None
        for r in range(4):
            part = lags[24 * r : 24 * r + 24]
            if (r - t) % 4:
                part = pltpu.roll(part, (r - t) % 4 * 32, 1)
            out = part if out is None else jnp.where(lane == r, part, out)
        for j in range(4):
            for g in range(6):
                piece_ref[j ^ chan, t : t + 1, g * 128 : (g + 1) * 128] = out[6 * j + g : 6 * j + g + 1]


def network_part(spectra, blocks):
    lag_dev = LAGS // 4
    shape = jax.ShapeDtypeStruct((2, TMPL, lag_dev), jnp.float32)
    return pl.pallas_call(
        network_kernel,
        out_shape=(shape, shape),
        in_specs=[VMEM] * 9,
        out_specs=(VMEM, VMEM),
        scratch_shapes=[
            pltpu.VMEM((8, 2, ROWS, 128), jnp.float32),
            pltpu.VMEM((4, TMPL, lag_dev), jnp.float32),
        ],
        compiler_params=PARAMS,
    )(spectra, *blocks, *tables())


def on_device(data_spec, tmpl_spec, shifts, mask):
    raw = data_spec.transpose(0, 2, 1)
    code = (shifts + NFFT * mask).astype(jnp.float32)
    dense, wide = early_part(raw, code)
    one, far = gather_xz(dense, from_offset(raw, dx=1), from_offset(raw, dy=2))
    blocks = gather_xy(one, far)
    spectra = template_part(tmpl_spec, wide, one)
    keep, send = network_part(spectra, blocks)
    got = lax.ppermute(send, "chan", [(i, i ^ 1) for i in range(4)])
    other = lax.ppermute(keep[1] + got[1], "chan", [(i, i ^ 2) for i in range(4)])
    return keep[0] + got[0] + other


def solution(mesh):
    return jax.shard_map(
        on_device,
        mesh=mesh,
        in_specs=(
            P(None, "chan", "tmpl"),
            P(None, "tmpl", "chan", None),
            P("tmpl", "chan"),
            P("tmpl", "chan"),
        ),
        out_specs=P("tmpl", "chan"),
        check_vma=False,
    )
```

```python
import functools
import math

import jax
import jax.numpy as jnp
import numpy as np
from jax import lax
from jax.experimental import pallas as pl
from jax.experimental.pallas import tpu as pltpu
from jax.sharding import PartitionSpec as P

FREQS = 1024
FIRST = 128
NFFT = 4096
LAGS = 3072
CHANS = 150
ROWS = 152
TMPL = 4
XH, YS, ZS = 2, 4, 8

VMEM = pl.BlockSpec(memory_space=pltpu.VMEM)
HIGH = lax.Precision.HIGHEST
PARAMS = pltpu.CompilerParams(vmem_limit_bytes=16 << 20)
LARGE = pltpu.CompilerParams(vmem_limit_bytes=45 << 20)


def from_offset(x, dx=0, dy=0, dz=0):
    pairs = []
    for i in range(XH * YS * ZS):
        a, b, c = i // (YS * ZS), i // ZS % YS, i % ZS
        for chan in range(4):
            turn = -dz if chan % 2 == 0 else dz
            src = (a + dx) % XH * (YS * ZS) + (b + dy) % YS * ZS + (c + turn) % ZS
            pairs.append((src * 4 + chan, i * 4 + chan))
    return lax.ppermute(x, ("tmpl", "chan"), pairs)


def half_turn_fit():
    x = np.cos(np.pi * (np.arange(400) + 0.5) / 400) * 0.25 + 0.25
    r = np.sqrt(x)
    even = np.polynomial.Chebyshev.fit(x, np.cos(np.pi * r), 5, domain=[0, 0.5])
    odd = np.polynomial.Chebyshev.fit(x, np.sin(np.pi * r) / r, 5, domain=[0, 0.5])
    return [[float(v) for v in p.convert(kind=np.polynomial.Polynomial).coef] for p in (even, odd)]


COS_FIT, SIN_FIT = half_turn_fit()


def sincos(turns):
    near = jnp.floor(turns + 0.5)
    r = turns - near
    half = near * 0.5
    sign = 1.0 - 4.0 * (half - jnp.floor(half))
    sq = r * r
    c, s = COS_FIT[-1], SIN_FIT[-1]
    for a, b in zip(COS_FIT[-2::-1], SIN_FIT[-2::-1]):
        c, s = c * sq + a, s * sq + b
    return sign, c, s * r


STEP = 50
STEPS = CHANS // STEP


def template_kernel(spec_hbm, wide_ref, after_hbm, out_ref, spec_ref, weight_ref, sems):
    def part(i):
        at = pl.ds(i * STEP, STEP)
        return [pltpu.make_async_copy(spec_hbm.at[k, at], spec_ref.at[k, at], sems.at[i, k]) for k in range(2)]

    for copy in part(0) + part(1):
        copy.start()
    row = lax.broadcasted_iota(jnp.int32, (8, 128), 0)
    lane = lax.broadcasted_iota(jnp.int32, (8, 128), 1)
    first_bin = (FIRST * (row // 4 + 1) + lane).astype(jnp.float32) * (2.0 / NFFT)

    def weigh(c):
        power = None
        for m in range(4):
            re, im = spec_ref[0, c, m], spec_ref[1, c, m]
            one = re * re + im * im
            power = one if power is None else power + one
        power = power + pltpu.roll(power, 4, 0)
        power = jnp.broadcast_to(jnp.sum(power, axis=1, keepdims=True), (8, 128))
        weight = lax.rsqrt(power * (1.0 / FREQS) + 1e-06)
        weight_ref[c] = jnp.where(wide_ref[c, 0] >= NFFT, weight, 0.0)

    def phase(c):
        sign, er, ei = sincos(first_bin * wide_ref[c, 0])
        wr, wi = wide_ref[c, 1], wide_ref[c, 2]
        weight = weight_ref[c] * sign
        er, ei = er * weight, ei * weight
        for m in range(4):
            re, im = spec_ref[0, c, m], spec_ref[1, c, m]
            out_ref[c, 0, m] = re * er + im * ei
            out_ref[c, 1, m] = re * ei - im * er
            if m < 3:
                er, ei = er * wr - ei * wi, er * wi + ei * wr

    for i in range(STEPS):
        for copy in part(i):
            copy.wait()
        if i + 2 < STEPS:
            for copy in part(i + 2):
                copy.start()
        for body, unroll in ((weigh, 25), (phase, 10)):

            def step(j, carry, body=body, unroll=unroll, i=i):
                for k in range(unroll):
                    body(i * STEP + j * unroll + k)
                return carry

            lax.fori_loop(0, STEP // unroll, step, 0)


def template_view(tmpl_spec):
    view = tmpl_spec.reshape(2, TMPL, CHANS, 4, 2, 128).transpose(0, 2, 3, 4, 1, 5)
    return view.reshape(2, CHANS, 4, 8, 128)


def template_part(tmpl_spec, wide, after):
    return pl.pallas_call(
        template_kernel,
        out_shape=jax.ShapeDtypeStruct((CHANS, 2, 4, 8, 128), jnp.float32),
        in_specs=[pl.BlockSpec(memory_space=pl.ANY), VMEM, pl.BlockSpec(memory_space=pl.ANY)],
        out_specs=VMEM,
        scratch_shapes=[
            pltpu.VMEM((2, CHANS, 4, 8, 128), jnp.float32),
            pltpu.VMEM((CHANS, 8, 128), jnp.float32),
            pltpu.SemaphoreType.DMA((STEPS, 2)),
        ],
        compiler_params=LARGE,
    )(template_view(tmpl_spec), wide, after)


REST = CHANS - 128
HELD = 3
REST_AT = HELD * 32
DENSE = REST_AT + 24


def put(j, ref, k, out_ref):
    out_ref[16 * j : 16 * j + 16, :] = ref[k, :, 0:128]
    if j < 4:
        out_ref[REST_AT : REST_AT + 16, 32 * j : 32 * j + REST] = ref[k, :, 128:CHANS]
        return
    for half in range(2):
        lanes = 64 * half + 32 * k
        out_ref[DENSE - 8 : DENSE, lanes : lanes + REST] = ref[k, 8 * half : 8 * half + 8, 128:CHANS]


def early_kernel(raw_ref, code_ref, own_ref, wide_ref, pair_ref):
    own_ref[...] = jnp.zeros((DENSE, 128), jnp.float32)
    for k in range(2):
        put(k, raw_ref, k, own_ref)
    pair_ref[0:4, 0:CHANS] = code_ref[...]
    pair_ref[4:8, 0:CHANS] = code_ref[...]
    for start in (0, 128):
        codes = pair_ref[:, start : start + 128]
        sign, wr, wi = sincos(codes * (2.0 * 2 * FIRST / NFFT))
        wr, wi = wr * sign, wi * sign
        for at in range(min(128, CHANS - start)):
            for k, part in enumerate((codes, wr, wi)):
                wide_ref[start + at, k] = jnp.broadcast_to(part[:, at : at + 1], (8, 128))


def early_part(raw, code):
    return pl.pallas_call(
        early_kernel,
        out_shape=(
            jax.ShapeDtypeStruct((DENSE, 128), jnp.float32),
            jax.ShapeDtypeStruct((CHANS, 3, 8, 128), jnp.float32),
        ),
        in_specs=[VMEM] * 2,
        out_specs=(VMEM, VMEM),
        scratch_shapes=[pltpu.VMEM((8, 256), jnp.float32)],
        compiler_params=PARAMS,
    )(raw, code)


def dense_kernel(own_ref, other_ref, far_ref, out_ref):
    out_ref[...] = own_ref[...]
    for k in range(2):
        put(2 + k, other_ref, k, out_ref)
        put(4 + k, far_ref, k, out_ref)


Z_ORDER = (0, 1, -1, 2, -2, 3, 4, -3)


def pack_kernel(*refs):
    parts, one_ref, far_ref, held = refs[:8], refs[8], refs[9], refs[10]
    z = lax.axis_index("tmpl") % ZS
    turn = 2 * (lax.axis_index("chan") % 2) - 1
    for part, dz in zip(parts, Z_ORDER):
        at = pl.multiple_of(lax.rem(z + turn * dz + ZS, ZS) * 16, 16)
        for j in range(REST_AT // 16 + 1):
            held[j, pl.ds(at, 16), :] = part[16 * j : 16 * j + 16, :]
        late = part[DENSE - 8 : DENSE, :]
        held[REST_AT // 16 + 1, pl.ds(at, 8), :] = late
        held[REST_AT // 16 + 1, pl.ds(at + 8, 8), :] = pltpu.roll(late, 64, 1)
    rest = [held[j].T for j in range(REST_AT // 16, REST_AT // 16 + 2)]
    for j in range(2 * HELD):
        out = one_ref.at[j // 2, j % 2] if j < 4 else far_ref.at[j % 2]
        out[0:128, :] = held[j].T
        out[128:ROWS, :] = rest[j // 4][32 * (j % 4) : 32 * (j % 4) + ROWS - 128]


def gather_xz(dense, other, far):
    own = pl.pallas_call(
        dense_kernel,
        out_shape=jax.ShapeDtypeStruct((DENSE, 128), jnp.float32),
        in_specs=[VMEM] * 3,
        out_specs=VMEM,
        compiler_params=PARAMS,
    )(dense, other, far)
    up = from_offset(own, dz=1)
    down = from_offset(own, dz=-1)
    up2 = from_offset(own, dz=2)
    down2 = from_offset(own, dz=-2)
    up3 = from_offset(up2, dz=1)
    up4 = from_offset(up2, dz=2)
    down3 = from_offset(down2, dz=-1)
    return pl.pallas_call(
        pack_kernel,
        out_shape=(
            jax.ShapeDtypeStruct((2, 2, ROWS, 128), jnp.float32),
            jax.ShapeDtypeStruct((2, ROWS, 128), jnp.float32),
        ),
        in_specs=[VMEM] * 8,
        out_specs=(VMEM, VMEM),
        scratch_shapes=[pltpu.VMEM((REST_AT // 16 + 2, 128, 128), jnp.float32)],
        compiler_params=PARAMS,
    )(own, up, down, up2, down2, up3, up4, down3)


def gather_xy(one, far):
    return one, from_offset(one, dy=1), from_offset(one, dy=-1), far, from_offset(far, dx=1)


def tables():
    kl = np.arange(32)
    fh = np.arange(8)
    a = 2 * np.pi * (np.outer(kl, fh + 1) % 32) / 32
    first = np.zeros((2, TMPL, 32, 2, 4, 2, TMPL))
    for t in range(TMPL):
        c, s = np.cos(a).reshape(32, 4, 2), np.sin(a).reshape(32, 4, 2)
        first[0, t, :, 0, :, :, t] = c
        first[0, t, :, 1, :, :, t] = -s
        first[1, t, :, 0, :, :, t] = s
        first[1, t, :, 1, :, :, t] = c
    fl = np.arange(128)
    b = np.tile(2 * np.pi * np.outer(kl, fl) / NFFT, (TMPL, 1))
    kh = (4 * np.arange(24)[None, :] + np.arange(4)[:, None]).reshape(96)
    g = 2 * np.pi * (np.outer(kh, fl) % 128) / 128
    rows = [first.reshape(256, 64)]
    twist = np.stack([np.cos(b), np.sin(b)])
    last = np.stack([np.cos(g), -np.sin(g)]) / FREQS
    return tuple(np.asarray(v, np.float32) for v in (rows[0], twist, last))


def network_kernel(*refs):
    spec_ref, (one_ref, up_ref, down_ref, far_ref, other_far_ref) = refs[0], refs[1:6]
    first_ref, twist_ref, last_ref = refs[6:9]
    out_refs, (data_ref, piece_ref) = refs[9:13], refs[13:]
    me = lax.axis_index("tmpl")
    x, y = me // (YS * ZS), me // ZS % YS

    views = [(ref.at[dx], dx, dy) for ref, dy in ((one_ref, 0), (up_ref, 1), (down_ref, YS - 1)) for dx in range(XH)]
    views += [(far_ref, 0, 2), (other_far_ref, 1, 2)]
    power = None
    for block, _, _ in views:
        re, im = block[0], block[1]
        part = re * re + im * im
        power = part if power is None else power + part
    power = jnp.sum(power, axis=1, keepdims=True)
    scale = jnp.broadcast_to(lax.rsqrt(power * (1.0 / FREQS) + 1e-06), (ROWS, 128))
    for block, dx, dy in views:
        group = lax.rem(x + dx, XH) * YS + lax.rem(y + dy, YS)
        for k in range(2):
            data_ref[group, k] = block[k] * scale

    lower = lax.broadcasted_iota(jnp.int32, (8, 128), 0) < 4

    def channel(c, acc):
        acc = list(acc)
        for m in range(4):
            d = []
            for k in range(2):
                one = jnp.broadcast_to(data_ref[2 * m, k, pl.ds(c, 1), :], (8, 128))
                two = jnp.broadcast_to(data_ref[2 * m + 1, k, pl.ds(c, 1), :], (8, 128))
                d.append(jnp.where(lower, one, two))
            tr, ti = spec_ref[c, 0, m], spec_ref[c, 1, m]
            acc[m] = acc[m] + (tr * d[0] - ti * d[1])
            acc[4 + m] = acc[4 + m] + (tr * d[1] + ti * d[0])
        return tuple(acc)

    acc = lax.fori_loop(0, CHANS, channel, (jnp.zeros((8, 128), jnp.float32),) * 8, unroll=15)
    to_lags(acc, first_ref, twist_ref, last_ref, piece_ref)
    for j, out_ref in enumerate(out_refs):
        out_ref[...] = piece_ref[j]


def to_lags(acc, first_ref, twist_ref, last_ref, piece_ref):
    spectra = jnp.concatenate(acc, axis=0)
    mixed = jnp.dot(first_ref[...], spectra, precision=HIGH, preferred_element_type=jnp.float32)
    yr, yi = mixed[0:128], mixed[128:256]
    tc, ts = twist_ref[0], twist_ref[1]
    zr, zi = yr * tc - yi * ts, yr * ts + yi * tc
    dims = (((1,), (1,)), ((), ()))
    lags = lax.dot_general(last_ref[0], zr, dims, precision=HIGH, preferred_element_type=jnp.float32)
    lags = lags + lax.dot_general(last_ref[1], zi, dims, precision=HIGH, preferred_element_type=jnp.float32)
    lane = lax.broadcasted_iota(jnp.int32, (24, 128), 1) // 32
    chan = lax.axis_index("chan")
    for t in range(TMPL):
        out = None
        for r in range(4):
            part = lags[24 * r : 24 * r + 24]
            if (r - t) % 4:
                part = pltpu.roll(part, (r - t) % 4 * 32, 1)
            out = part if out is None else jnp.where(lane == r, part, out)
        for j in range(4):
            for g in range(6):
                piece_ref[j ^ chan, t : t + 1, g * 128 : (g + 1) * 128] = out[6 * j + g : 6 * j + g + 1]


def network_part(spectra, blocks):
    lag_dev = LAGS // 4
    shape = jax.ShapeDtypeStruct((TMPL, lag_dev), jnp.float32)
    return pl.pallas_call(
        network_kernel,
        out_shape=(shape,) * 4,
        in_specs=[VMEM] * 9,
        out_specs=(VMEM,) * 4,
        scratch_shapes=[
            pltpu.VMEM((8, 2, ROWS, 128), jnp.float32),
            pltpu.VMEM((4, TMPL, lag_dev), jnp.float32),
        ],
        compiler_params=PARAMS,
    )(spectra, *blocks, *tables())


def on_device(data_spec, tmpl_spec, shifts, mask):
    raw = data_spec.transpose(0, 2, 1)
    code = (shifts + NFFT * mask).astype(jnp.float32)
    dense, wide = early_part(raw, code)
    one, far = gather_xz(dense, from_offset(raw, dx=1), from_offset(raw, dy=2))
    blocks = gather_xy(one, far)
    spectra = template_part(tmpl_spec, wide, one)
    pieces = network_part(spectra, blocks)
    got = [lax.ppermute(pieces[j], "chan", [(i, i ^ j) for i in range(4)]) for j in (3, 2, 1)]
    return pieces[0] + got[2] + (got[1] + got[0])


def solution(mesh):
    return jax.shard_map(
        on_device,
        mesh=mesh,
        in_specs=(
            P(None, "chan", "tmpl"),
            P(None, "tmpl", "chan", None),
            P("tmpl", "chan"),
            P("tmpl", "chan"),
        ),
        out_specs=P("tmpl", "chan"),
        check_vma=False,
    )
```

```python
import functools
import math

import jax
import jax.numpy as jnp
import numpy as np
from jax import lax
from jax.experimental import pallas as pl
from jax.experimental.pallas import tpu as pltpu
from jax.sharding import PartitionSpec as P

FREQS = 1024
FIRST = 128
NFFT = 4096
LAGS = 3072
CHANS = 150
ROWS = 152
TMPL = 4
XH, YS, ZS = 2, 4, 8

VMEM = pl.BlockSpec(memory_space=pltpu.VMEM)
HIGH = lax.Precision.HIGH
PARAMS = pltpu.CompilerParams(vmem_limit_bytes=16 << 20)
LARGE = pltpu.CompilerParams(vmem_limit_bytes=45 << 20)


def from_offset(x, dx=0, dy=0, dz=0):
    pairs = []
    for i in range(XH * YS * ZS):
        a, b, c = i // (YS * ZS), i // ZS % YS, i % ZS
        for chan in range(4):
            turn = -dz if chan % 2 == 0 else dz
            src = (a + dx) % XH * (YS * ZS) + (b + dy) % YS * ZS + (c + turn) % ZS
            pairs.append((src * 4 + chan, i * 4 + chan))
    return lax.ppermute(x, ("tmpl", "chan"), pairs)


def half_turn_fit():
    x = np.cos(np.pi * (np.arange(400) + 0.5) / 400) * 0.25 + 0.25
    r = np.sqrt(x)
    even = np.polynomial.Chebyshev.fit(x, np.cos(np.pi * r), 5, domain=[0, 0.5])
    odd = np.polynomial.Chebyshev.fit(x, np.sin(np.pi * r) / r, 5, domain=[0, 0.5])
    return [[float(v) for v in p.convert(kind=np.polynomial.Polynomial).coef] for p in (even, odd)]


COS_FIT, SIN_FIT = half_turn_fit()


def sincos(turns):
    near = jnp.floor(turns + 0.5)
    r = turns - near
    half = near * 0.5
    sign = 1.0 - 4.0 * (half - jnp.floor(half))
    sq = r * r
    c, s = COS_FIT[-1], SIN_FIT[-1]
    for a, b in zip(COS_FIT[-2::-1], SIN_FIT[-2::-1]):
        c, s = c * sq + a, s * sq + b
    return sign, c, s * r


STEP = 50
STEPS = CHANS // STEP


def template_kernel(spec_hbm, wide_ref, after_hbm, out_ref, spec_ref, weight_ref, sems):
    def part(i):
        at = pl.ds(i * STEP, STEP)
        return [pltpu.make_async_copy(spec_hbm.at[k, at], spec_ref.at[k, at], sems.at[i, k]) for k in range(2)]

    for copy in part(0) + part(1):
        copy.start()
    row = lax.broadcasted_iota(jnp.int32, (8, 128), 0)
    lane = lax.broadcasted_iota(jnp.int32, (8, 128), 1)
    first_bin = (FIRST * (row // 4 + 1) + lane).astype(jnp.float32) * (2.0 / NFFT)

    def weigh(c):
        power = None
        for m in range(4):
            re, im = spec_ref[0, c, m], spec_ref[1, c, m]
            one = re * re + im * im
            power = one if power is None else power + one
        power = power + pltpu.roll(power, 4, 0)
        power = jnp.broadcast_to(jnp.sum(power, axis=1, keepdims=True), (8, 128))
        weight = lax.rsqrt(power * (1.0 / FREQS) + 1e-06)
        weight_ref[c] = jnp.where(wide_ref[c, 0] >= NFFT, weight, 0.0)

    def phase(c):
        sign, er, ei = sincos(first_bin * wide_ref[c, 0])
        wr, wi = wide_ref[c, 1], wide_ref[c, 2]
        weight = weight_ref[c] * sign
        er, ei = er * weight, ei * weight
        for m in range(4):
            re, im = spec_ref[0, c, m], spec_ref[1, c, m]
            out_ref[c, 0, m] = re * er + im * ei
            out_ref[c, 1, m] = re * ei - im * er
            if m < 3:
                er, ei = er * wr - ei * wi, er * wi + ei * wr

    for i in range(STEPS):
        for copy in part(i):
            copy.wait()
        if i + 2 < STEPS:
            for copy in part(i + 2):
                copy.start()
        for body, unroll in ((weigh, 25), (phase, 10)):

            def step(j, carry, body=body, unroll=unroll, i=i):
                for k in range(unroll):
                    body(i * STEP + j * unroll + k)
                return carry

            lax.fori_loop(0, STEP // unroll, step, 0)


def template_view(tmpl_spec):
    view = tmpl_spec.reshape(2, TMPL, CHANS, 4, 2, 128).transpose(0, 2, 3, 4, 1, 5)
    return view.reshape(2, CHANS, 4, 8, 128)


def template_part(tmpl_spec, wide, after):
    return pl.pallas_call(
        template_kernel,
        out_shape=jax.ShapeDtypeStruct((CHANS, 2, 4, 8, 128), jnp.float32),
        in_specs=[pl.BlockSpec(memory_space=pl.ANY), VMEM, pl.BlockSpec(memory_space=pl.ANY)],
        out_specs=VMEM,
        scratch_shapes=[
            pltpu.VMEM((2, CHANS, 4, 8, 128), jnp.float32),
            pltpu.VMEM((CHANS, 8, 128), jnp.float32),
            pltpu.SemaphoreType.DMA((STEPS, 2)),
        ],
        compiler_params=LARGE,
    )(template_view(tmpl_spec), wide, after)


REST = CHANS - 128
HELD = 3
REST_AT = HELD * 32
DENSE = REST_AT + 24


def put(j, ref, k, out_ref):
    out_ref[16 * j : 16 * j + 16, :] = ref[k, :, 0:128]
    if j < 4:
        out_ref[REST_AT : REST_AT + 16, 32 * j : 32 * j + REST] = ref[k, :, 128:CHANS]
        return
    for half in range(2):
        lanes = 64 * half + 32 * k
        out_ref[DENSE - 8 : DENSE, lanes : lanes + REST] = ref[k, 8 * half : 8 * half + 8, 128:CHANS]


def early_kernel(raw_ref, code_ref, own_ref, wide_ref, pair_ref):
    own_ref[...] = jnp.zeros((DENSE, 128), jnp.float32)
    for k in range(2):
        put(k, raw_ref, k, own_ref)
    pair_ref[0:4, 0:CHANS] = code_ref[...]
    pair_ref[4:8, 0:CHANS] = code_ref[...]
    for start in (0, 128):
        codes = pair_ref[:, start : start + 128]
        sign, wr, wi = sincos(codes * (2.0 * 2 * FIRST / NFFT))
        wr, wi = wr * sign, wi * sign
        for at in range(min(128, CHANS - start)):
            for k, part in enumerate((codes, wr, wi)):
                wide_ref[start + at, k] = jnp.broadcast_to(part[:, at : at + 1], (8, 128))


def early_part(raw, code):
    return pl.pallas_call(
        early_kernel,
        out_shape=(
            jax.ShapeDtypeStruct((DENSE, 128), jnp.float32),
            jax.ShapeDtypeStruct((CHANS, 3, 8, 128), jnp.float32),
        ),
        in_specs=[VMEM] * 2,
        out_specs=(VMEM, VMEM),
        scratch_shapes=[pltpu.VMEM((8, 256), jnp.float32)],
        compiler_params=PARAMS,
    )(raw, code)


def dense_kernel(own_ref, other_ref, far_ref, out_ref):
    out_ref[...] = own_ref[...]
    for k in range(2):
        put(2 + k, other_ref, k, out_ref)
        put(4 + k, far_ref, k, out_ref)


Z_ORDER = (0, -1, 1, 2, -2, 3, 4, -3)


def pack_kernel(*refs):
    parts, one_ref, far_ref, held = refs[:8], refs[8], refs[9], refs[10]
    z = lax.axis_index("tmpl") % ZS
    turn = 2 * (lax.axis_index("chan") % 2) - 1
    for part, dz in zip(parts, Z_ORDER):
        at = pl.multiple_of(lax.rem(z + turn * dz + ZS, ZS) * 16, 16)
        for j in range(REST_AT // 16 + 1):
            held[j, pl.ds(at, 16), :] = part[16 * j : 16 * j + 16, :]
        late = part[DENSE - 8 : DENSE, :]
        held[REST_AT // 16 + 1, pl.ds(at, 8), :] = late
        held[REST_AT // 16 + 1, pl.ds(at + 8, 8), :] = pltpu.roll(late, 64, 1)
    rest = [held[j].T for j in range(REST_AT // 16, REST_AT // 16 + 2)]
    for j in range(2 * HELD):
        out = one_ref.at[j // 2, j % 2] if j < 4 else far_ref.at[j % 2]
        out[0:128, :] = held[j].T
        out[128:ROWS, :] = rest[j // 4][32 * (j % 4) : 32 * (j % 4) + ROWS - 128]


def gather_xz(dense, other, far):
    own = pl.pallas_call(
        dense_kernel,
        out_shape=jax.ShapeDtypeStruct((DENSE, 128), jnp.float32),
        in_specs=[VMEM] * 3,
        out_specs=VMEM,
        compiler_params=PARAMS,
    )(dense, other, far)
    up = from_offset(own, dz=1)
    down = from_offset(own, dz=-1)
    up2 = from_offset(own, dz=2)
    down2 = from_offset(own, dz=-2)
    up3 = from_offset(up2, dz=1)
    up4 = from_offset(up2, dz=2)
    down3 = from_offset(down2, dz=-1)
    return pl.pallas_call(
        pack_kernel,
        out_shape=(
            jax.ShapeDtypeStruct((2, 2, ROWS, 128), jnp.float32),
            jax.ShapeDtypeStruct((2, ROWS, 128), jnp.float32),
        ),
        in_specs=[VMEM] * 8,
        out_specs=(VMEM, VMEM),
        scratch_shapes=[pltpu.VMEM((REST_AT // 16 + 2, 128, 128), jnp.float32)],
        compiler_params=PARAMS,
    )(own, down, up, up2, down2, up3, up4, down3)


def gather_xy(one, far):
    return one, from_offset(one, dy=1), from_offset(one, dy=-1), far, from_offset(far, dx=1)


def tables():
    kl = np.arange(32)
    fh = np.arange(8)
    a = 2 * np.pi * (np.outer(kl, fh + 1) % 32) / 32
    first = np.zeros((2, TMPL, 32, 2, 4, 2, TMPL))
    for t in range(TMPL):
        c, s = np.cos(a).reshape(32, 4, 2), np.sin(a).reshape(32, 4, 2)
        first[0, t, :, 0, :, :, t] = c
        first[0, t, :, 1, :, :, t] = -s
        first[1, t, :, 0, :, :, t] = s
        first[1, t, :, 1, :, :, t] = c
    fl = np.arange(128)
    b = np.tile(2 * np.pi * np.outer(kl, fl) / NFFT, (TMPL, 1))
    kh = (4 * np.arange(24)[None, :] + np.arange(4)[:, None]).reshape(96)
    g = 2 * np.pi * (np.outer(kh, fl) % 128) / 128
    rows = [first.reshape(256, 64)]
    twist = np.stack([np.cos(b), np.sin(b)])
    last = np.stack([np.cos(g), -np.sin(g)]) / FREQS
    return tuple(np.asarray(v, np.float32) for v in (rows[0], twist, last))


def network_kernel(*refs):
    spec_ref, (one_ref, up_ref, down_ref, far_ref, other_far_ref) = refs[0], refs[1:6]
    first_ref, twist_ref, last_ref = refs[6:9]
    out_refs, (data_ref, piece_ref) = refs[9:13], refs[13:]
    me = lax.axis_index("tmpl")
    x, y = me // (YS * ZS), me // ZS % YS

    views = [(ref.at[dx], dx, dy) for ref, dy in ((one_ref, 0), (up_ref, 1), (down_ref, YS - 1)) for dx in range(XH)]
    views += [(far_ref, 0, 2), (other_far_ref, 1, 2)]
    power = None
    for block, _, _ in views:
        re, im = block[0], block[1]
        part = re * re + im * im
        power = part if power is None else power + part
    power = jnp.sum(power, axis=1, keepdims=True)
    scale = jnp.broadcast_to(lax.rsqrt(power * (1.0 / FREQS) + 1e-06), (ROWS, 128))
    for block, dx, dy in views:
        group = lax.rem(x + dx, XH) * YS + lax.rem(y + dy, YS)
        for k in range(2):
            data_ref[group, k] = block[k] * scale

    lower = lax.broadcasted_iota(jnp.int32, (8, 128), 0) < 4

    def channel(c, acc):
        acc = list(acc)
        for m in range(4):
            d = []
            for k in range(2):
                one = jnp.broadcast_to(data_ref[2 * m, k, pl.ds(c, 1), :], (8, 128))
                two = jnp.broadcast_to(data_ref[2 * m + 1, k, pl.ds(c, 1), :], (8, 128))
                d.append(jnp.where(lower, one, two))
            tr, ti = spec_ref[c, 0, m], spec_ref[c, 1, m]
            acc[m] = acc[m] + (tr * d[0] - ti * d[1])
            acc[4 + m] = acc[4 + m] + (tr * d[1] + ti * d[0])
        return tuple(acc)

    acc = lax.fori_loop(0, CHANS, channel, (jnp.zeros((8, 128), jnp.float32),) * 8, unroll=15)
    to_lags(acc, first_ref, twist_ref, last_ref, piece_ref)
    for j, out_ref in enumerate(out_refs):
        out_ref[...] = piece_ref[j]


def to_lags(acc, first_ref, twist_ref, last_ref, piece_ref):
    spectra = jnp.concatenate(acc, axis=0)
    mixed = jnp.dot(first_ref[...], spectra, precision=HIGH, preferred_element_type=jnp.float32)
    yr, yi = mixed[0:128], mixed[128:256]
    tc, ts = twist_ref[0], twist_ref[1]
    zr, zi = yr * tc - yi * ts, yr * ts + yi * tc
    dims = (((1,), (1,)), ((), ()))
    lags = lax.dot_general(last_ref[0], zr, dims, precision=HIGH, preferred_element_type=jnp.float32)
    lags = lags + lax.dot_general(last_ref[1], zi, dims, precision=HIGH, preferred_element_type=jnp.float32)
    lane = lax.broadcasted_iota(jnp.int32, (24, 128), 1) // 32
    chan = lax.axis_index("chan")
    for t in range(TMPL):
        out = None
        for r in range(4):
            part = lags[24 * r : 24 * r + 24]
            if (r - t) % 4:
                part = pltpu.roll(part, (r - t) % 4 * 32, 1)
            out = part if out is None else jnp.where(lane == r, part, out)
        for j in range(4):
            for g in range(6):
                piece_ref[j ^ chan, t : t + 1, g * 128 : (g + 1) * 128] = out[6 * j + g : 6 * j + g + 1]


def network_part(spectra, blocks):
    lag_dev = LAGS // 4
    shape = jax.ShapeDtypeStruct((TMPL, lag_dev), jnp.float32)
    return pl.pallas_call(
        network_kernel,
        out_shape=(shape,) * 4,
        in_specs=[VMEM] * 9,
        out_specs=(VMEM,) * 4,
        scratch_shapes=[
            pltpu.VMEM((8, 2, ROWS, 128), jnp.float32),
            pltpu.VMEM((4, TMPL, lag_dev), jnp.float32),
        ],
        compiler_params=PARAMS,
    )(spectra, *blocks, *tables())


def on_device(data_spec, tmpl_spec, shifts, mask):
    raw = data_spec.transpose(0, 2, 1)
    code = (shifts + NFFT * mask).astype(jnp.float32)
    dense, wide = early_part(raw, code)
    one, far = gather_xz(dense, from_offset(raw, dx=1), from_offset(raw, dy=2))
    blocks = gather_xy(one, far)
    spectra = template_part(tmpl_spec, wide, one)
    pieces = network_part(spectra, blocks)
    got = [lax.ppermute(pieces[j], "chan", [(i, i ^ j) for i in range(4)]) for j in (3, 2, 1)]
    return pieces[0] + got[2] + (got[1] + got[0])


def solution(mesh):
    return jax.shard_map(
        on_device,
        mesh=mesh,
        in_specs=(
            P(None, "chan", "tmpl"),
            P(None, "tmpl", "chan", None),
            P("tmpl", "chan"),
            P("tmpl", "chan"),
        ),
        out_specs=P("tmpl", "chan"),
        check_vma=False,
    )
```

```python
import functools
import math

import jax
import jax.numpy as jnp
import numpy as np
from jax import lax
from jax.experimental import pallas as pl
from jax.experimental.pallas import tpu as pltpu
from jax.sharding import PartitionSpec as P

FREQS = 1024
FIRST = 128
NFFT = 4096
LAGS = 3072
CHANS = 150
ROWS = 152
TMPL = 4
XH, YS, ZS = 2, 4, 8

VMEM = pl.BlockSpec(memory_space=pltpu.VMEM)
HIGH = lax.Precision.HIGH
PARAMS = pltpu.CompilerParams(vmem_limit_bytes=16 << 20)
LARGE = pltpu.CompilerParams(vmem_limit_bytes=45 << 20)


def from_offset(x, dx=0, dy=0, dz=0):
    pairs = []
    for i in range(XH * YS * ZS):
        a, b, c = i // (YS * ZS), i // ZS % YS, i % ZS
        for chan in range(4):
            turn = -dz
            src = (a + dx) % XH * (YS * ZS) + (b + dy) % YS * ZS + (c + turn) % ZS
            pairs.append((src * 4 + chan, i * 4 + chan))
    return lax.ppermute(x, ("tmpl", "chan"), pairs)


def half_turn_fit():
    x = np.cos(np.pi * (np.arange(400) + 0.5) / 400) * 0.25 + 0.25
    r = np.sqrt(x)
    even = np.polynomial.Chebyshev.fit(x, np.cos(np.pi * r), 5, domain=[0, 0.5])
    odd = np.polynomial.Chebyshev.fit(x, np.sin(np.pi * r) / r, 5, domain=[0, 0.5])
    return [[float(v) for v in p.convert(kind=np.polynomial.Polynomial).coef] for p in (even, odd)]


COS_FIT, SIN_FIT = half_turn_fit()


def sincos(turns):
    near = jnp.floor(turns + 0.5)
    r = turns - near
    half = near * 0.5
    sign = 1.0 - 4.0 * (half - jnp.floor(half))
    sq = r * r
    c, s = COS_FIT[-1], SIN_FIT[-1]
    for a, b in zip(COS_FIT[-2::-1], SIN_FIT[-2::-1]):
        c, s = c * sq + a, s * sq + b
    return sign, c, s * r


STEP = 50
STEPS = CHANS // STEP


def template_kernel(spec_hbm, wide_ref, after_hbm, out_ref, spec_ref, weight_ref, sems):
    def part(i):
        at = pl.ds(i * STEP, STEP)
        return [pltpu.make_async_copy(spec_hbm.at[k, at], spec_ref.at[k, at], sems.at[i, k]) for k in range(2)]

    for copy in part(0) + part(1):
        copy.start()
    row = lax.broadcasted_iota(jnp.int32, (8, 128), 0)
    lane = lax.broadcasted_iota(jnp.int32, (8, 128), 1)
    first_bin = (FIRST * (row // 4 + 1) + lane).astype(jnp.float32) * (2.0 / NFFT)

    def weigh(c):
        power = None
        for m in range(4):
            re, im = spec_ref[0, c, m], spec_ref[1, c, m]
            one = re * re + im * im
            power = one if power is None else power + one
        power = power + pltpu.roll(power, 4, 0)
        power = jnp.broadcast_to(jnp.sum(power, axis=1, keepdims=True), (8, 128))
        weight = lax.rsqrt(power * (1.0 / FREQS) + 1e-06)
        weight_ref[c] = jnp.where(wide_ref[c, 0] >= NFFT, weight, 0.0)

    def phase(c):
        sign, er, ei = sincos(first_bin * wide_ref[c, 0])
        wr, wi = wide_ref[c, 1], wide_ref[c, 2]
        weight = weight_ref[c] * sign
        er, ei = er * weight, ei * weight
        for m in range(4):
            re, im = spec_ref[0, c, m], spec_ref[1, c, m]
            out_ref[c, 0, m] = re * er + im * ei
            out_ref[c, 1, m] = re * ei - im * er
            if m < 3:
                er, ei = er * wr - ei * wi, er * wi + ei * wr

    for i in range(STEPS):
        for copy in part(i):
            copy.wait()
        if i + 2 < STEPS:
            for copy in part(i + 2):
                copy.start()
        for body, unroll in ((weigh, 25), (phase, 10)):

            def step(j, carry, body=body, unroll=unroll, i=i):
                for k in range(unroll):
                    body(i * STEP + j * unroll + k)
                return carry

            lax.fori_loop(0, STEP // unroll, step, 0)


def template_view(tmpl_spec):
    view = tmpl_spec.reshape(2, TMPL, CHANS, 4, 2, 128).transpose(0, 2, 3, 4, 1, 5)
    return view.reshape(2, CHANS, 4, 8, 128)


def template_part(tmpl_spec, wide, after):
    return pl.pallas_call(
        template_kernel,
        out_shape=jax.ShapeDtypeStruct((CHANS, 2, 4, 8, 128), jnp.float32),
        in_specs=[pl.BlockSpec(memory_space=pl.ANY), VMEM, pl.BlockSpec(memory_space=pl.ANY)],
        out_specs=VMEM,
        scratch_shapes=[
            pltpu.VMEM((2, CHANS, 4, 8, 128), jnp.float32),
            pltpu.VMEM((CHANS, 8, 128), jnp.float32),
            pltpu.SemaphoreType.DMA((STEPS, 2)),
        ],
        compiler_params=LARGE,
    )(template_view(tmpl_spec), wide, after)


REST = CHANS - 128
HELD = 3
REST_AT = HELD * 32
DENSE = REST_AT + 24


def put(j, ref, k, out_ref):
    out_ref[16 * j : 16 * j + 16, :] = ref[k, :, 0:128]
    if j < 4:
        out_ref[REST_AT : REST_AT + 16, 32 * j : 32 * j + REST] = ref[k, :, 128:CHANS]
        return
    for half in range(2):
        lanes = 64 * half + 32 * k
        out_ref[DENSE - 8 : DENSE, lanes : lanes + REST] = ref[k, 8 * half : 8 * half + 8, 128:CHANS]


def early_kernel(raw_ref, code_ref, own_ref, wide_ref, pair_ref):
    own_ref[...] = jnp.zeros((DENSE, 128), jnp.float32)
    for k in range(2):
        put(k, raw_ref, k, own_ref)
    pair_ref[0:4, 0:CHANS] = code_ref[...]
    pair_ref[4:8, 0:CHANS] = code_ref[...]
    for start in (0, 128):
        codes = pair_ref[:, start : start + 128]
        sign, wr, wi = sincos(codes * (2.0 * 2 * FIRST / NFFT))
        wr, wi = wr * sign, wi * sign
        for at in range(min(128, CHANS - start)):
            for k, part in enumerate((codes, wr, wi)):
                wide_ref[start + at, k] = jnp.broadcast_to(part[:, at : at + 1], (8, 128))


def early_part(raw, code):
    return pl.pallas_call(
        early_kernel,
        out_shape=(
            jax.ShapeDtypeStruct((DENSE, 128), jnp.float32),
            jax.ShapeDtypeStruct((CHANS, 3, 8, 128), jnp.float32),
        ),
        in_specs=[VMEM] * 2,
        out_specs=(VMEM, VMEM),
        scratch_shapes=[pltpu.VMEM((8, 256), jnp.float32)],
        compiler_params=PARAMS,
    )(raw, code)


def dense_kernel(own_ref, other_ref, far_ref, out_ref):
    out_ref[...] = own_ref[...]
    for k in range(2):
        put(2 + k, other_ref, k, out_ref)
        put(4 + k, far_ref, k, out_ref)


Z_ORDER = (0, -1, 1, 2, -2, 3, 4, -3)


def pack_kernel(*refs):
    parts, one_ref, far_ref, held = refs[:8], refs[8], refs[9], refs[10]
    z = lax.axis_index("tmpl") % ZS
    turn = -1
    for part, dz in zip(parts, Z_ORDER):
        at = pl.multiple_of(lax.rem(z + turn * dz + ZS, ZS) * 16, 16)
        for j in range(REST_AT // 16 + 1):
            held[j, pl.ds(at, 16), :] = part[16 * j : 16 * j + 16, :]
        late = part[DENSE - 8 : DENSE, :]
        held[REST_AT // 16 + 1, pl.ds(at, 8), :] = late
        held[REST_AT // 16 + 1, pl.ds(at + 8, 8), :] = pltpu.roll(late, 64, 1)
    rest = [held[j].T for j in range(REST_AT // 16, REST_AT // 16 + 2)]
    for j in range(2 * HELD):
        out = one_ref.at[j // 2, j % 2] if j < 4 else far_ref.at[j % 2]
        out[0:128, :] = held[j].T
        out[128:ROWS, :] = rest[j // 4][32 * (j % 4) : 32 * (j % 4) + ROWS - 128]


def gather_xz(dense, other, far):
    own = pl.pallas_call(
        dense_kernel,
        out_shape=jax.ShapeDtypeStruct((DENSE, 128), jnp.float32),
        in_specs=[VMEM] * 3,
        out_specs=VMEM,
        compiler_params=PARAMS,
    )(dense, other, far)
    up = from_offset(own, dz=1)
    down = from_offset(own, dz=-1)
    up2 = from_offset(own, dz=2)
    down2 = from_offset(own, dz=-2)
    up3 = from_offset(up2, dz=1)
    up4 = from_offset(up2, dz=2)
    down3 = from_offset(down2, dz=-1)
    return pl.pallas_call(
        pack_kernel,
        out_shape=(
            jax.ShapeDtypeStruct((2, 2, ROWS, 128), jnp.float32),
            jax.ShapeDtypeStruct((2, ROWS, 128), jnp.float32),
        ),
        in_specs=[VMEM] * 8,
        out_specs=(VMEM, VMEM),
        scratch_shapes=[pltpu.VMEM((REST_AT // 16 + 2, 128, 128), jnp.float32)],
        compiler_params=PARAMS,
    )(own, down, up, up2, down2, up3, up4, down3)


def gather_xy(one, far):
    return one, from_offset(one, dy=1), from_offset(one, dy=-1), far, from_offset(far, dx=1)


def tables():
    kl = np.arange(32)
    fh = np.arange(8)
    a = 2 * np.pi * (np.outer(kl, fh + 1) % 32) / 32
    first = np.zeros((2, TMPL, 32, 2, 4, 2, TMPL))
    for t in range(TMPL):
        c, s = np.cos(a).reshape(32, 4, 2), np.sin(a).reshape(32, 4, 2)
        first[0, t, :, 0, :, :, t] = c
        first[0, t, :, 1, :, :, t] = -s
        first[1, t, :, 0, :, :, t] = s
        first[1, t, :, 1, :, :, t] = c
    fl = np.arange(128)
    b = np.tile(2 * np.pi * np.outer(kl, fl) / NFFT, (TMPL, 1))
    kh = (4 * np.arange(24)[None, :] + np.arange(4)[:, None]).reshape(96)
    g = 2 * np.pi * (np.outer(kh, fl) % 128) / 128
    rows = [first.reshape(256, 64)]
    twist = np.stack([np.cos(b), np.sin(b)])
    last = np.stack([np.cos(g), -np.sin(g)]) / FREQS
    return tuple(np.asarray(v, np.float32) for v in (rows[0], twist, last))


def network_kernel(*refs):
    spec_ref, (one_ref, up_ref, down_ref, far_ref, other_far_ref) = refs[0], refs[1:6]
    first_ref, twist_ref, last_ref = refs[6:9]
    out_refs, (data_ref, piece_ref) = refs[9:13], refs[13:]
    me = lax.axis_index("tmpl")
    x, y = me // (YS * ZS), me // ZS % YS

    views = [(ref.at[dx], dx, dy) for ref, dy in ((one_ref, 0), (up_ref, 1), (down_ref, YS - 1)) for dx in range(XH)]
    views += [(far_ref, 0, 2), (other_far_ref, 1, 2)]
    power = None
    for block, _, _ in views:
        re, im = block[0], block[1]
        part = re * re + im * im
        power = part if power is None else power + part
    power = jnp.sum(power, axis=1, keepdims=True)
    scale = jnp.broadcast_to(lax.rsqrt(power * (1.0 / FREQS) + 1e-06), (ROWS, 128))
    for block, dx, dy in views:
        group = lax.rem(x + dx, XH) * YS + lax.rem(y + dy, YS)
        for k in range(2):
            data_ref[group, k] = block[k] * scale

    lower = lax.broadcasted_iota(jnp.int32, (8, 128), 0) < 4

    def channel(c, acc):
        acc = list(acc)
        for m in range(4):
            d = []
            for k in range(2):
                one = jnp.broadcast_to(data_ref[2 * m, k, pl.ds(c, 1), :], (8, 128))
                two = jnp.broadcast_to(data_ref[2 * m + 1, k, pl.ds(c, 1), :], (8, 128))
                d.append(jnp.where(lower, one, two))
            tr, ti = spec_ref[c, 0, m], spec_ref[c, 1, m]
            acc[m] = acc[m] + (tr * d[0] - ti * d[1])
            acc[4 + m] = acc[4 + m] + (tr * d[1] + ti * d[0])
        return tuple(acc)

    acc = lax.fori_loop(0, CHANS, channel, (jnp.zeros((8, 128), jnp.float32),) * 8, unroll=15)
    to_lags(acc, first_ref, twist_ref, last_ref, piece_ref)
    for j, out_ref in enumerate(out_refs):
        out_ref[...] = piece_ref[j]


def to_lags(acc, first_ref, twist_ref, last_ref, piece_ref):
    spectra = jnp.concatenate(acc, axis=0)
    mixed = jnp.dot(first_ref[...], spectra, precision=HIGH, preferred_element_type=jnp.float32)
    yr, yi = mixed[0:128], mixed[128:256]
    tc, ts = twist_ref[0], twist_ref[1]
    zr, zi = yr * tc - yi * ts, yr * ts + yi * tc
    dims = (((1,), (1,)), ((), ()))
    lags = lax.dot_general(last_ref[0], zr, dims, precision=HIGH, preferred_element_type=jnp.float32)
    lags = lags + lax.dot_general(last_ref[1], zi, dims, precision=HIGH, preferred_element_type=jnp.float32)
    lane = lax.broadcasted_iota(jnp.int32, (24, 128), 1) // 32
    chan = lax.axis_index("chan")
    for t in range(TMPL):
        out = None
        for r in range(4):
            part = lags[24 * r : 24 * r + 24]
            if (r - t) % 4:
                part = pltpu.roll(part, (r - t) % 4 * 32, 1)
            out = part if out is None else jnp.where(lane == r, part, out)
        for j in range(4):
            for g in range(6):
                piece_ref[j ^ chan, t : t + 1, g * 128 : (g + 1) * 128] = out[6 * j + g : 6 * j + g + 1]


def network_part(spectra, blocks):
    lag_dev = LAGS // 4
    shape = jax.ShapeDtypeStruct((TMPL, lag_dev), jnp.float32)
    return pl.pallas_call(
        network_kernel,
        out_shape=(shape,) * 4,
        in_specs=[VMEM] * 9,
        out_specs=(VMEM,) * 4,
        scratch_shapes=[
            pltpu.VMEM((8, 2, ROWS, 128), jnp.float32),
            pltpu.VMEM((4, TMPL, lag_dev), jnp.float32),
        ],
        compiler_params=PARAMS,
    )(spectra, *blocks, *tables())


def on_device(data_spec, tmpl_spec, shifts, mask):
    raw = data_spec.transpose(0, 2, 1)
    code = (shifts + NFFT * mask).astype(jnp.float32)
    dense, wide = early_part(raw, code)
    one, far = gather_xz(dense, from_offset(raw, dx=1), from_offset(raw, dy=2))
    blocks = gather_xy(one, far)
    spectra = template_part(tmpl_spec, wide, one)
    pieces = network_part(spectra, blocks)
    got = [lax.ppermute(pieces[j], "chan", [(i, i ^ j) for i in range(4)]) for j in (1, 2, 3)]
    return pieces[0] + got[0] + (got[1] + got[2])


def solution(mesh):
    return jax.shard_map(
        on_device,
        mesh=mesh,
        in_specs=(
            P(None, "chan", "tmpl"),
            P(None, "tmpl", "chan", None),
            P("tmpl", "chan"),
            P("tmpl", "chan"),
        ),
        out_specs=P("tmpl", "chan"),
        check_vma=False,
    )
```
